32 devices in a mesh: group: 2 (over x), dp: 8 (over z, y), mp: 2 (over core).
Axes of the slice: x: 2, y: 2, z: 4, core: 2. Of those that a mesh axis runs over, the one named last changes fastest.
Arguments:
- teacher_hidden: bfloat16 [1024, 8192], P('dp', ('group', 'mp')), may hold values from -6 to 6
- teacher_gain: bfloat16 [8192], P(('group', 'mp')), may hold values from 0.25 to 1.75
- teacher_head: bfloat16 [8192, 8192], P(('group', 'mp')), may hold values from -0.198873782 to 0.198873782
- student_hidden: bfloat16 [1024, 4096], P('dp'), may hold values from -6 to 6
- student_head: bfloat16 [4096, 8192], P('dp', ('group', 'mp')), may hold values from -0.28125 to 0.28125
- depth_cut: int32 [16], P('dp'), may hold values from 1 to 4
Outputs:
- kl_terms: float32 [4, 1024], P(None, 'dp')
- hidden_grad: float32 [1024, 4096], P('dp', ('group', 'mp'))
- head_grad: float32 [4096, 8192], P('dp', ('group', 'mp'))
The draws below stay inside these ranges and needn't reach their ends.
Inputs may be any that keep to these rules, and one draw needn't show every extreme that they name: `depth_cut`: each sample's number of codebooks kept.
All inputs are finite; a program needn't handle non-finite values.
Results may differ from the reference program's by a relative error of at most 0.0053.
Values may be sent and summed in bfloat16 or wider, within the bound.
A program may use at most 192 MiB of HBM per device.

```python
import jax
import jax.numpy as jnp
from jax import lax

DT = 8192
DS = 4096
C = 4
V = 2048
FRAMES = 64
TOKENS = 1024
SAMPLES = 16


def drawn_rows(key, salt_code, feature_count):
    noise_key = jax.random.fold_in(key, salt_code)
    return jnp.clip(jax.random.normal(noise_key, (TOKENS, feature_count), jnp.float32), -6.0, 6.0)


def drawn_head(key, salt_code, feature_count):
    noise_key = jax.random.fold_in(key, salt_code)
    normal_values = jnp.clip(jax.random.normal(noise_key, (feature_count, C * V), jnp.float32), -6.0, 6.0)
    return normal_values * (3.0 * feature_count ** (-0.5))


def draw_teacher_hidden(key, part):
    values = drawn_rows(key, 101, DT)
    return values.astype(jnp.bfloat16)


def draw_student_hidden(key, part):
    values = drawn_rows(key, 103, DS)
    return values.astype(jnp.bfloat16)


def draw_teacher_head(key, part):
    values = drawn_head(key, 102, DT)
    return values.astype(jnp.bfloat16)


def draw_student_head(key, part):
    values = drawn_head(key, 104, DS)
    return values.astype(jnp.bfloat16)


def place_ends(values, rng, low, largest):
    longest = values.shape.index(max(values.shape))
    spots = []
    for shift in (0, 1):
        where = [jax.random.randint(jax.random.fold_in(rng, axis), (), 0, length) for axis, length in enumerate(values.shape)]
        where[longest] = (where[longest] + shift) % values.shape[longest]
        spots.append(tuple(where))
    return values.at[spots[0]].set(low).at[spots[1]].set(largest)


def setup_inputs(seed: int = 0) -> dict:
    seeds = jax.random.split(jax.random.key(seed), 7)
    return {
        "teacher_hidden": draw_teacher_hidden(jax.random.fold_in(seeds[6], 71), 0),
        "teacher_gain": jnp.clip(1.0 + 0.15 * jax.random.normal(seeds[1], (DT,), jnp.float32), 0.25, 1.75).astype(jnp.bfloat16),
        "teacher_head": draw_teacher_head(jax.random.fold_in(seeds[6], 71), 0),
        "student_hidden": draw_student_hidden(jax.random.fold_in(seeds[6], 71), 0),
        "student_head": draw_student_head(jax.random.fold_in(seeds[6], 71), 0),
        "depth_cut": place_ends(jax.random.randint(seeds[5], (SAMPLES,), 1, C + 1), jax.random.fold_in(seeds[5], 1), 1, C).astype(jnp.int32),
    }


epsilon = 1e-05

def reference(teacher_hidden, teacher_gain, teacher_head, student_hidden, student_head, depth_cut):
    hidden_float = teacher_hidden.astype(jnp.float32)
    squares = lax.optimization_barrier(jnp.mean(hidden_float * hidden_float, axis=1, keepdims=True))
    normed = (hidden_float * lax.rsqrt(squares + epsilon) * teacher_gain.astype(jnp.float32)[None, :]).astype(jnp.bfloat16)
    teacher_scores = jnp.dot(normed, teacher_head, preferred_element_type=jnp.float32).reshape(TOKENS, C, V)
    student_scores = jnp.dot(student_hidden, student_head, preferred_element_type=jnp.float32).reshape(TOKENS, C, V)
    teacher_log = jax.nn.log_softmax(teacher_scores, axis=2)
    student_log = jax.nn.log_softmax(student_scores, axis=2)
    teacher_prob = jnp.exp(teacher_log)
    divergence = lax.optimization_barrier(jnp.sum(teacher_prob * (teacher_log - student_log), axis=2))
    depth_rows = jnp.repeat(depth_cut, FRAMES)
    alive_mask = (jnp.arange(C, dtype=jnp.int32)[None, :] < depth_rows[:, None]).astype(jnp.float32)
    depth_weight = alive_mask / depth_rows[:, None].astype(jnp.float32)
    kl_terms = (divergence * depth_weight).T
    score_grad = ((jnp.exp(student_log) - teacher_prob) * depth_weight[:, :, None]).reshape(TOKENS, C * V).astype(jnp.bfloat16)
    hidden_grad = jnp.dot(score_grad, student_head.T, preferred_element_type=jnp.float32)
    head_grad = jnp.dot(student_hidden.T, score_grad, preferred_element_type=jnp.float32)
    return (kl_terms, hidden_grad, head_grad)
```

```python
import jax
import jax.numpy as jnp
from jax import lax
from jax.sharding import PartitionSpec as P

C = 4
FRAMES = 64
PARTS = ("group", "mp")


epsilon = 1e-05


def book_share(values, op, share):
    every = lax.all_gather(values[:, 0], PARTS, axis=0)
    own = lax.axis_index(PARTS) // share
    block = lax.dynamic_slice_in_dim(every, own * share, share, 0)
    return op(block, axis=0)[:, None]


def shards(teacher_hidden, teacher_gain, teacher_head, student_hidden, student_head, depth_cut):
    part_count = lax.axis_size(PARTS)
    part = lax.axis_index(PARTS)
    frame_count = teacher_hidden.shape[0]
    row_parts = lax.axis_size("dp")
    columns = student_head.shape[1]
    entries = columns * part_count // C
    feature_total = teacher_hidden.shape[1] * part_count

    blocks = student_hidden.reshape(frame_count, row_parts, -1).transpose(1, 0, 2)
    hidden_columns = lax.all_to_all(blocks, "dp", split_axis=0, concat_axis=0, tiled=True)
    hidden_columns = hidden_columns.reshape(frame_count * row_parts, -1)
    student_part = jnp.dot(hidden_columns, student_head, preferred_element_type=jnp.float32)
    student_part, hidden_columns, teacher_hidden = lax.optimization_barrier(
        (student_part, hidden_columns, teacher_hidden)
    )
    student_scores = lax.psum_scatter(student_part, "dp", scatter_dimension=0, tiled=True)
    hidden_rows = lax.optimization_barrier(hidden_columns.T)

    hidden_float = teacher_hidden.astype(jnp.float32)
    squares = lax.psum(jnp.sum(hidden_float * hidden_float, axis=1), PARTS)
    row_scale = lax.rsqrt(squares / feature_total + epsilon)
    normed = (hidden_float * row_scale[:, None] * teacher_gain.astype(jnp.float32)[None, :]).astype(
        jnp.bfloat16
    )
    teacher_scores = lax.psum_scatter(
        jnp.dot(normed, teacher_head, preferred_element_type=jnp.float32),
        PARTS,
        scatter_dimension=1,
        tiled=True,
    )

    depth_rows = jnp.repeat(depth_cut, FRAMES)
    books = max(columns // entries, 1)
    share = max(entries // columns, 1)
    book_range = jnp.arange(books, dtype=jnp.int32) + part * books // share
    alive_mask = (book_range[None, :] < depth_rows[:, None]).astype(jnp.float32)
    depth_weight = alive_mask / depth_rows[:, None].astype(jnp.float32)

    def log_softmax(scores):
        top = jnp.max(scores, axis=-1, keepdims=True)
        if share > 1:
            top = book_share(top, jnp.max, share)
        shifted = scores - top
        total = jnp.sum(jnp.exp(shifted), axis=-1, keepdims=True)
        if share > 1:
            total = book_share(total, jnp.sum, share)
        return shifted - jnp.log(total)

    grads = []
    terms = []
    width = columns // books
    for book in range(books):
        span = slice(book * width, (book + 1) * width)
        weight = depth_weight[:, book : book + 1]
        teacher_log = log_softmax(teacher_scores[:, span])
        student_log = log_softmax(student_scores[:, span])
        teacher_prob = jnp.exp(teacher_log)
        divergence = jnp.sum(teacher_prob * (teacher_log - student_log), axis=-1, keepdims=True)
        grads.append(((jnp.exp(student_log) - teacher_prob) * weight).astype(jnp.bfloat16))
        terms.append((divergence * weight)[:, 0])
    score_grad = grads[0] if books == 1 else jnp.concatenate(grads, axis=1)
    every_term = lax.all_gather(jnp.stack(terms), PARTS, axis=0, tiled=True)
    kl_terms = jnp.sum(every_term.reshape(C, share, frame_count), axis=1)

    every_grad = lax.all_gather(score_grad, "dp", axis=0, tiled=True)
    hidden_part = lax.dot_general(
        every_grad, student_head, (((1,), (1,)), ((), ())), preferred_element_type=jnp.float32
    ).astype(jnp.bfloat16)
    hidden_part = hidden_part.reshape(row_parts, frame_count, -1)
    hidden_part = lax.all_to_all(hidden_part, "dp", split_axis=0, concat_axis=0, tiled=True)
    hidden_part = hidden_part.reshape(part_count, row_parts // part_count, frame_count, -1)
    hidden_part = lax.all_to_all(hidden_part, PARTS, split_axis=0, concat_axis=0, tiled=True)
    hidden_sum = jnp.sum(hidden_part.astype(jnp.float32), axis=0)
    hidden_grad = hidden_sum.transpose(1, 0, 2).reshape(frame_count, -1)
    head_grad = jnp.dot(hidden_rows, every_grad, preferred_element_type=jnp.float32)
    return (kl_terms, hidden_grad, head_grad)


def solution(mesh):
    return jax.shard_map(
        shards,
        mesh=mesh,
        in_specs=(
            P("dp", PARTS),
            P(PARTS),
            P(PARTS, None),
            P("dp", None),
            P("dp", PARTS),
            P("dp"),
        ),
        out_specs=(P(None, "dp"), P("dp", PARTS), P("dp", PARTS)),
        check_vma=False,
    )
```

```python
import jax
import jax.numpy as jnp
from jax import lax
from jax.sharding import PartitionSpec as P

C = 4
FRAMES = 64
PARTS = ("group", "mp")


epsilon = 1e-05


def book_share(values, op, share):
    every = lax.all_gather(values[:, 0], PARTS, axis=0)
    own = lax.axis_index(PARTS) // share
    block = lax.dynamic_slice_in_dim(every, own * share, share, 0)
    return op(block, axis=0)[:, None]


def shards(teacher_hidden, teacher_gain, teacher_head, student_hidden, student_head, depth_cut):
    part_count = lax.axis_size(PARTS)
    part = lax.axis_index(PARTS)
    frame_count = teacher_hidden.shape[0]
    row_parts = lax.axis_size("dp")
    columns = student_head.shape[1]
    entries = columns * part_count // C
    feature_total = teacher_hidden.shape[1] * part_count

    blocks = student_hidden.reshape(frame_count, row_parts, -1).transpose(1, 0, 2)
    hidden_columns = lax.all_to_all(blocks, "dp", split_axis=0, concat_axis=0, tiled=True)
    hidden_columns = hidden_columns.reshape(frame_count * row_parts, -1)
    student_part = jnp.dot(hidden_columns, student_head, preferred_element_type=jnp.float32)
    student_part, hidden_columns, teacher_hidden = lax.optimization_barrier(
        (student_part, hidden_columns, teacher_hidden)
    )
    student_scores = lax.psum_scatter(student_part, "dp", scatter_dimension=0, tiled=True)
    hidden_rows = lax.optimization_barrier(hidden_columns.T)

    hidden_float = teacher_hidden.astype(jnp.float32)
    squares = lax.psum(jnp.sum(hidden_float * hidden_float, axis=1), PARTS)
    row_scale = lax.rsqrt(squares / feature_total + epsilon)
    normed = (hidden_float * row_scale[:, None] * teacher_gain.astype(jnp.float32)[None, :]).astype(
        jnp.bfloat16
    )
    teacher_part = jnp.dot(normed, teacher_head, preferred_element_type=jnp.float32)
    teacher_part = teacher_part.reshape(frame_count, part_count, columns).transpose(1, 0, 2)
    teacher_part = lax.all_to_all(teacher_part, PARTS, split_axis=0, concat_axis=0, tiled=True)
    teacher_scores = jnp.sum(teacher_part, axis=0)

    depth_rows = jnp.repeat(depth_cut, FRAMES)
    books = max(columns // entries, 1)
    share = max(entries // columns, 1)
    book_range = jnp.arange(books, dtype=jnp.int32) + part * books // share
    alive_mask = (book_range[None, :] < depth_rows[:, None]).astype(jnp.float32)
    depth_weight = alive_mask / depth_rows[:, None].astype(jnp.float32)

    def log_softmax(scores):
        top = jnp.max(scores, axis=-1, keepdims=True)
        if share > 1:
            top = book_share(top, jnp.max, share)
        shifted = scores - top
        total = jnp.sum(jnp.exp(shifted), axis=-1, keepdims=True)
        if share > 1:
            total = book_share(total, jnp.sum, share)
        return shifted - jnp.log(total)

    grads = []
    terms = []
    width = columns // books
    for book in range(books):
        span = slice(book * width, (book + 1) * width)
        weight = depth_weight[:, book : book + 1]
        teacher_log = log_softmax(teacher_scores[:, span])
        student_log = log_softmax(student_scores[:, span])
        teacher_prob = jnp.exp(teacher_log)
        divergence = jnp.sum(teacher_prob * (teacher_log - student_log), axis=-1, keepdims=True)
        grads.append(((jnp.exp(student_log) - teacher_prob) * weight).astype(jnp.bfloat16))
        terms.append((divergence * weight)[:, 0])
    score_grad = grads[0] if books == 1 else jnp.concatenate(grads, axis=1)
    every_term = lax.all_gather(jnp.stack(terms), PARTS, axis=0, tiled=True)
    kl_terms = jnp.sum(every_term.reshape(C, share, frame_count), axis=1)

    every_grad = lax.all_gather(score_grad, "dp", axis=0, tiled=True)
    every_grad, kl_terms = lax.optimization_barrier((every_grad, kl_terms))
    hidden_part = lax.dot_general(
        every_grad, student_head, (((1,), (1,)), ((), ())), preferred_element_type=jnp.float32
    ).astype(jnp.bfloat16)
    hidden_part = hidden_part.reshape(row_parts, frame_count, -1)
    hidden_part = lax.all_to_all(hidden_part, "dp", split_axis=0, concat_axis=0, tiled=True)
    head_grad = jnp.dot(hidden_rows, every_grad, preferred_element_type=jnp.float32)
    hidden_part, head_grad = lax.optimization_barrier((hidden_part, head_grad))
    hidden_part = hidden_part.reshape(part_count, row_parts // part_count, frame_count, -1)
    hidden_part = lax.all_to_all(hidden_part, PARTS, split_axis=0, concat_axis=0, tiled=True)
    hidden_sum = jnp.sum(hidden_part.astype(jnp.float32), axis=0)
    hidden_grad = hidden_sum.transpose(1, 0, 2).reshape(frame_count, -1)
    return (kl_terms, hidden_grad, head_grad)


def solution(mesh):
    return jax.shard_map(
        shards,
        mesh=mesh,
        in_specs=(
            P("dp", PARTS),
            P(PARTS),
            P(PARTS, None),
            P("dp", None),
            P("dp", PARTS),
            P("dp"),
        ),
        out_specs=(P(None, "dp"), P("dp", PARTS), P("dp", PARTS)),
        check_vma=False,
    )
```

```python
import jax
import jax.numpy as jnp
from jax import lax
from jax.sharding import PartitionSpec as P

C = 4
FRAMES = 64
PARTS = ("group", "mp")


epsilon = 1e-05


def book_share(values, op, share):
    every = lax.all_gather(values[:, 0], PARTS, axis=0)
    own = lax.axis_index(PARTS) // share
    block = lax.dynamic_slice_in_dim(every, own * share, share, 0)
    return op(block, axis=0)[:, None]


def shards(teacher_hidden, teacher_gain, teacher_head, student_hidden, student_head, depth_cut):
    part_count = lax.axis_size(PARTS)
    part = lax.axis_index(PARTS)
    frame_count = teacher_hidden.shape[0]
    row_parts = lax.axis_size("dp")
    columns = student_head.shape[1]
    entries = columns * part_count // C
    feature_total = teacher_hidden.shape[1] * part_count

    blocks = student_hidden.reshape(frame_count, row_parts, -1).transpose(1, 0, 2)
    hidden_columns = lax.all_to_all(blocks, "dp", split_axis=0, concat_axis=0, tiled=True)
    hidden_columns = hidden_columns.reshape(frame_count * row_parts, -1)
    student_part = jnp.dot(hidden_columns, student_head, preferred_element_type=jnp.float32)
    student_part, hidden_columns, teacher_hidden = lax.optimization_barrier(
        (student_part, hidden_columns, teacher_hidden)
    )
    student_scores = lax.psum_scatter(student_part, "dp", scatter_dimension=0, tiled=True)
    half = frame_count // 2
    halves = hidden_columns.reshape(row_parts, 2, half, -1)
    hidden_rows = lax.optimization_barrier(
        [halves[:, k].reshape(half * row_parts, -1).T for k in range(2)]
    )

    hidden_float = teacher_hidden.astype(jnp.float32)
    squares = lax.psum(jnp.sum(hidden_float * hidden_float, axis=1), PARTS)
    row_scale = lax.rsqrt(squares / feature_total + epsilon)
    normed = (hidden_float * row_scale[:, None] * teacher_gain.astype(jnp.float32)[None, :]).astype(
        jnp.bfloat16
    )
    teacher_part = jnp.dot(normed, teacher_head, preferred_element_type=jnp.float32)
    teacher_part = teacher_part.reshape(frame_count, part_count, columns).transpose(1, 0, 2)
    teacher_part = lax.all_to_all(teacher_part, PARTS, split_axis=0, concat_axis=0, tiled=True)
    teacher_scores = jnp.sum(teacher_part, axis=0)

    depth_rows = jnp.repeat(depth_cut, FRAMES)
    books = max(columns // entries, 1)
    share = max(entries // columns, 1)
    book_range = jnp.arange(books, dtype=jnp.int32) + part * books // share
    alive_mask = (book_range[None, :] < depth_rows[:, None]).astype(jnp.float32)
    depth_weight = alive_mask / depth_rows[:, None].astype(jnp.float32)

    def log_softmax(scores):
        top = jnp.max(scores, axis=-1, keepdims=True)
        if share > 1:
            top = book_share(top, jnp.max, share)
        shifted = scores - top
        total = jnp.sum(jnp.exp(shifted), axis=-1, keepdims=True)
        if share > 1:
            total = book_share(total, jnp.sum, share)
        return shifted - jnp.log(total)

    grads = []
    terms = []
    width = columns // books
    for book in range(books):
        span = slice(book * width, (book + 1) * width)
        weight = depth_weight[:, book : book + 1]
        teacher_log = log_softmax(teacher_scores[:, span])
        student_log = log_softmax(student_scores[:, span])
        teacher_prob = jnp.exp(teacher_log)
        divergence = jnp.sum(teacher_prob * (teacher_log - student_log), axis=-1, keepdims=True)
        grads.append(((jnp.exp(student_log) - teacher_prob) * weight).astype(jnp.bfloat16))
        terms.append((divergence * weight)[:, 0])
    score_grad = grads[0] if books == 1 else jnp.concatenate(grads, axis=1)
    every_term = lax.all_gather(jnp.stack(terms), PARTS, axis=0, tiled=True)
    kl_terms = jnp.sum(every_term.reshape(C, share, frame_count), axis=1)

    first = lax.all_gather(score_grad[:half], "dp", axis=0, tiled=True)
    second = lax.all_gather(score_grad[half:], "dp", axis=0, tiled=True)

    def hidden_blocks(every_grad):
        block = lax.dot_general(
            every_grad, student_head, (((1,), (1,)), ((), ())), preferred_element_type=jnp.float32
        ).astype(jnp.bfloat16)
        block = block.reshape(row_parts, half, -1)
        return lax.all_to_all(block, "dp", split_axis=0, concat_axis=0, tiled=True)

    def hidden_sum(block):
        block = block.reshape(part_count, row_parts // part_count, half, -1)
        block = lax.all_to_all(block, PARTS, split_axis=0, concat_axis=0, tiled=True)
        total = jnp.sum(block.astype(jnp.float32), axis=0)
        return total.transpose(1, 0, 2).reshape(half, -1)

    first_hidden = hidden_sum(hidden_blocks(first))
    first_hidden, second, kl_terms = lax.optimization_barrier((first_hidden, second, kl_terms))
    second_blocks = hidden_blocks(second)
    head_grad = jnp.dot(hidden_rows[0], first, preferred_element_type=jnp.float32) + jnp.dot(
        hidden_rows[1], second, preferred_element_type=jnp.float32
    )
    second_blocks, head_grad = lax.optimization_barrier((second_blocks, head_grad))
    hidden_grad = jnp.concatenate([first_hidden, hidden_sum(second_blocks)], axis=0)
    return (kl_terms, hidden_grad, head_grad)


def solution(mesh):
    return jax.shard_map(
        shards,
        mesh=mesh,
        in_specs=(
            P("dp", PARTS),
            P(PARTS),
            P(PARTS, None),
            P("dp", None),
            P("dp", PARTS),
            P("dp"),
        ),
        out_specs=(P(None, "dp"), P("dp", PARTS), P("dp", PARTS)),
        check_vma=False,
    )
```

```python
import jax
import jax.numpy as jnp
from jax import lax
from jax.sharding import PartitionSpec as P

C = 4
FRAMES = 64
PARTS = ("group", "mp")


epsilon = 1e-05


def book_share(values, op, share):
    every = lax.all_gather(values[:, 0], PARTS, axis=0)
    own = lax.axis_index(PARTS) // share
    block = lax.dynamic_slice_in_dim(every, own * share, share, 0)
    return op(block, axis=0)[:, None]


def shards(teacher_hidden, teacher_gain, teacher_head, student_hidden, student_head, depth_cut):
    part_count = lax.axis_size(PARTS)
    part = lax.axis_index(PARTS)
    frame_count = teacher_hidden.shape[0]
    row_parts = lax.axis_size("dp")
    columns = student_head.shape[1]
    entries = columns * part_count // C
    feature_total = teacher_hidden.shape[1] * part_count

    blocks = student_hidden.reshape(frame_count, row_parts, -1).transpose(1, 0, 2)
    hidden_columns = lax.all_to_all(blocks, "dp", split_axis=0, concat_axis=0, tiled=True)
    hidden_columns = hidden_columns.reshape(frame_count * row_parts, -1)
    student_part = jnp.dot(hidden_columns, student_head, preferred_element_type=jnp.float32)
    student_part, hidden_columns, teacher_hidden = lax.optimization_barrier(
        (student_part, hidden_columns, teacher_hidden)
    )
    student_scores = lax.psum_scatter(student_part, "dp", scatter_dimension=0, tiled=True)
    hidden_rows = lax.optimization_barrier(hidden_columns.T)

    hidden_float = teacher_hidden.astype(jnp.float32)
    squares = lax.psum(jnp.sum(hidden_float * hidden_float, axis=1), PARTS)
    row_scale = lax.rsqrt(squares / feature_total + epsilon)
    normed = (hidden_float * row_scale[:, None] * teacher_gain.astype(jnp.float32)[None, :]).astype(
        jnp.bfloat16
    )
    teacher_part = jnp.dot(normed, teacher_head, preferred_element_type=jnp.float32)
    teacher_part = teacher_part.reshape(frame_count, part_count, columns).transpose(1, 0, 2)
    teacher_part = lax.all_to_all(teacher_part, PARTS, split_axis=0, concat_axis=0, tiled=True)
    teacher_scores = jnp.sum(teacher_part, axis=0)

    depth_rows = jnp.repeat(depth_cut, FRAMES)
    books = max(columns // entries, 1)
    share = max(entries // columns, 1)
    book_range = jnp.arange(books, dtype=jnp.int32) + part * books // share
    alive_mask = (book_range[None, :] < depth_rows[:, None]).astype(jnp.float32)
    depth_weight = alive_mask / depth_rows[:, None].astype(jnp.float32)

    def log_softmax(scores):
        top = jnp.max(scores, axis=-1, keepdims=True)
        if share > 1:
            top = book_share(top, jnp.max, share)
        shifted = scores - top
        total = jnp.sum(jnp.exp(shifted), axis=-1, keepdims=True)
        if share > 1:
            total = book_share(total, jnp.sum, share)
        return shifted - jnp.log(total)

    grads = []
    terms = []
    width = columns // books
    for book in range(books):
        span = slice(book * width, (book + 1) * width)
        weight = depth_weight[:, book : book + 1]
        teacher_log = log_softmax(teacher_scores[:, span])
        student_log = log_softmax(student_scores[:, span])
        teacher_prob = jnp.exp(teacher_log)
        divergence = jnp.sum(teacher_prob * (teacher_log - student_log), axis=-1, keepdims=True)
        grads.append(((jnp.exp(student_log) - teacher_prob) * weight).astype(jnp.bfloat16))
        terms.append((divergence * weight)[:, 0])
    score_grad = grads[0] if books == 1 else jnp.concatenate(grads, axis=1)
    every_term = lax.all_gather(jnp.stack(terms), PARTS, axis=0, tiled=True)
    kl_terms = jnp.sum(every_term.reshape(C, share, frame_count), axis=1)

    every_grad = lax.all_gather(score_grad, "dp", axis=0, tiled=True)
    every_grad, kl_terms = lax.optimization_barrier((every_grad, kl_terms))
    hidden_part = lax.dot_general(
        every_grad, student_head, (((1,), (1,)), ((), ())), preferred_element_type=jnp.float32
    ).astype(jnp.bfloat16)
    rounds = row_parts // part_count
    hidden_part = hidden_part.reshape(part_count, rounds * frame_count, -1)
    hidden_part = lax.all_to_all(hidden_part, PARTS, split_axis=0, concat_axis=0, tiled=True)
    head_grad = jnp.dot(hidden_rows, every_grad, preferred_element_type=jnp.float32)
    hidden_part, head_grad = lax.optimization_barrier((hidden_part, head_grad))
    hidden_sum = jnp.sum(hidden_part.astype(jnp.float32), axis=0).astype(jnp.bfloat16)
    hidden_sum = hidden_sum.reshape(rounds, frame_count, -1)
    row = lax.axis_index("dp")
    cores = lax.axis_size("mp")

    def spot(row_place, piece):
        return (piece // cores * row_parts + row_place) * cores + piece % cores

    arrived = []
    for turn in range(rounds):
        pairs = [
            (
                spot(source, piece),
                spot(rounds * piece + (turn + source) % rounds, source // rounds),
            )
            for source in range(row_parts)
            for piece in range(part_count)
        ]
        block = lax.dynamic_index_in_dim(hidden_sum, (turn + row) % rounds, 0, keepdims=False)
        arrived.append(lax.ppermute(block, ("group", "dp", "mp"), pairs))
    ordered = arrived
    if rounds > 1:
        stacked = jnp.stack(arrived)
        ordered = [
            lax.dynamic_index_in_dim(stacked, (row - slot + rounds) % rounds, 0, keepdims=False)
            for slot in range(rounds)
        ]
    hidden_grad = jnp.concatenate(ordered, axis=1).astype(jnp.float32)
    return (kl_terms, hidden_grad, head_grad)


def solution(mesh):
    return jax.shard_map(
        shards,
        mesh=mesh,
        in_specs=(
            P("dp", PARTS),
            P(PARTS),
            P(PARTS, None),
            P("dp", None),
            P("dp", PARTS),
            P("dp"),
        ),
        out_specs=(P(None, "dp"), P("dp", PARTS), P("dp", PARTS)),
        check_vma=False,
    )
```
